128 devices in a mesh: dp: 4 (over z), ctx: 32 (over x, y, core).
Axes of the slice: x: 4, y: 4, z: 4, core: 2. Of those that a mesh axis runs over, the one named last changes fastest.
Arguments:
- queries: bfloat16 [4, 4096, 4096], P('dp', 'ctx'), may hold values from -2.5 to 2.5
- key_state_vectors: bfloat16 [4, 4096, 512], P('dp', 'ctx'), may hold values from -2.5 to 2.5
- value_state_vectors: bfloat16 [4, 4096, 512], P('dp', 'ctx'), may hold values from -4 to 4
- output_gradient: bfloat16 [4, 4096, 4096], P('dp', 'ctx'), may hold values from -6 to 6
- lengths: int32 [4, 16], replicated, may hold values from 1 to 768, 4096 in all within a row
Outputs:
- grad_queries: bfloat16 [4, 4096, 4096], P('dp', 'ctx')
- grad_keys: bfloat16 [4, 4096, 512], P('dp', 'ctx')
- grad_values: bfloat16 [4, 4096, 512], P('dp', 'ctx')
The draws below stay inside these ranges and needn't reach their ends.
Inputs may be any that keep to these rules, and one draw needn't show every extreme that they name: Each row holds 16 document lengths that sum to 4096; the longest in each row is exactly 768.
All inputs are finite; a program needn't handle non-finite values.
Results may differ from the reference program's by a relative error of at most 0.0055.
Values may be sent and summed in bfloat16 or wider, within the bound.
A program may use at most 128 MiB of HBM per device.

```python
import math
import jax
import jax.numpy as jnp
import numpy as np
from jax import lax

QUERY_HEADS = 32
KEY_VALUE_HEADS = 4
HEAD_WIDTH = 128
GROUP_QUERIES = 8
TOKENS_PER_SHARD = 128
REACH = 7
BATCH_LENGTH = 4096
DOCS = 16
MAXDOC = 768
N_DP = 4


def steps_of(stream_key, extent, pieces, least, high):
    def one(axis_at, blocks):
        draws = jax.random.uniform(jax.random.fold_in(jax.random.fold_in(stream_key, 6), axis_at), (blocks,), jnp.float32, least / len(pieces), high / len(pieces))
        return jnp.repeat(jnp.exp(draws), extent[axis_at] // blocks).reshape((-1,) + (1,) * (len(extent) - axis_at - 1))

    gain = one(*pieces[0])
    for cut in pieces[1:]:
        gain = gain * one(*cut)
    return gain


def profile(count, total, bound, skew):
    weights = [(1 << 20) // math.isqrt(rank ** skew) + 1 for rank in range(2, count + 1)]
    surplus, given = total - bound - (count - 1), [1] * (count - 1)
    while surplus > 0:
        movable = [i for i in range(count - 1) if given[i] < bound]
        pool, left = sum([weights[i] for i in movable]), surplus
        for i in movable:
            more = min(bound - given[i], max(1, left * weights[i] // pool), surplus)
            given[i] = given[i] + more
            surplus = surplus - more
    return np.array([bound] + given)


def uneven(rng, number_of, total, limit, lean):
    if number_of == 2:
        one = jax.random.randint(rng, (), max(1, total - limit), min(limit, total - 1) + 1)
        return jnp.stack([one, total - one])
    sizes = jnp.asarray(profile(number_of, total, limit, lean), jnp.int32)
    couples = (number_of - 1) // 2
    source_of, receiver = sizes[1:1 + 2 * couples:2], sizes[2:2 + 2 * couples:2]
    room = jnp.minimum(source_of - 1, limit - receiver)
    passed = jax.random.randint(jax.random.fold_in(rng, 1), (couples,), 0, 1 << 20) % (room + 1)
    sizes = sizes.at[1:1 + 2 * couples:2].set(source_of - passed).at[2:2 + 2 * couples:2].set(receiver + passed)
    return sizes[jax.random.permutation(jax.random.fold_in(rng, 2), number_of)]


def scatter_about(own_key, extent, spread, bound, shards=(), kind=jnp.bfloat16):
    loudness = steps_of(own_key, extent, shards, -0.22, 0.18) if shards else 1.0
    array = jax.random.normal(own_key, extent, jnp.float32) * spread * loudness
    return jnp.minimum(jnp.maximum(array, -bound), bound).astype(kind)


def setup_inputs(seed: int = 0) -> dict:
    key_of = jax.random.split(jax.random.key(seed), 6)
    return {
        "queries": scatter_about(key_of[0], (N_DP, BATCH_LENGTH, QUERY_HEADS * HEAD_WIDTH), 1.0, 2.5, ((0, 4), (1, 32))),
        "key_state_vectors": scatter_about(key_of[1], (N_DP, BATCH_LENGTH, KEY_VALUE_HEADS * HEAD_WIDTH), 1.0, 2.5, ((0, 4), (1, 32))),
        "value_state_vectors": scatter_about(key_of[2], (N_DP, BATCH_LENGTH, KEY_VALUE_HEADS * HEAD_WIDTH), 1.0, 4.0, ((0, 4), (1, 32))),
        "output_gradient": scatter_about(key_of[3], (N_DP, BATCH_LENGTH, QUERY_HEADS * HEAD_WIDTH), 1.0, 6.0, ((0, 4), (1, 32))),
        "lengths": jax.vmap(lambda own: uneven(own, DOCS, BATCH_LENGTH, MAXDOC, 2))(jax.random.split(key_of[4], N_DP)).reshape((N_DP, DOCS)).astype(jnp.int32),
    }


def doc_index(doc_lengths, positions):
    bounds = jnp.cumsum(doc_lengths)
    return lax.optimization_barrier(jnp.sum((bounds[None, :] <= positions[:, None]).astype(jnp.int32), axis=1))

def pair_mask(doc_lengths, query_block, key_block, count_of_rows):
    offsets = jnp.arange(count_of_rows, dtype=jnp.int32)
    row_list = query_block * count_of_rows + offsets
    columns = key_block * count_of_rows + offsets
    same_doc = doc_index(doc_lengths, row_list)[:, None] == doc_index(doc_lengths, columns)[None, :]
    return same_doc & (columns[None, :] <= row_list[:, None]) & (key_block >= 0)

def to_low(values):
    return lax.optimization_barrier(values.astype(jnp.bfloat16)).astype(jnp.float32)

def forward_pair(query, key_part, value_part, visible, factor):
    scores = jnp.einsum('qgeh,kgh->qgek', query.astype(jnp.float32), key_part.astype(jnp.float32)) * factor
    weights = jnp.where(visible[:, None, None, :], jnp.exp(scores), 0.0)
    partial_value = jnp.einsum('qgek,kgh->qgeh', to_low(weights), value_part.astype(jnp.float32))
    return (lax.optimization_barrier(jnp.sum(weights, axis=-1)), partial_value)

def backward_pair(query, key_part, value_part, grad_out, visible, row_total, delta, factor):
    query_f = query.astype(jnp.float32)
    key_f = key_part.astype(jnp.float32)
    grad_f = grad_out.astype(jnp.float32)
    scores = jnp.einsum('qgeh,kgh->qgek', query_f, key_f) * factor
    probs = jnp.where(visible[:, None, None, :], jnp.exp(scores), 0.0) / row_total[..., None]
    grad_value = jnp.einsum('qgek,qgeh->kgh', to_low(probs), grad_f)
    grad_prob = jnp.einsum('qgeh,kgh->qgek', grad_f, value_part.astype(jnp.float32))
    grad_score = to_low(probs * (grad_prob - delta[..., None]))
    grad_query = jnp.einsum('qgek,kgh->qgeh', grad_score, key_f) * factor
    grad_key = jnp.einsum('qgek,qgeh->kgh', grad_score, query_f) * factor
    return (grad_query, grad_key, grad_value)

def one_batch(query_row_set, key_row_set, value_row_set, gradient_row_set, doc_lengths):
    block_list = query_row_set.shape[0] // TOKENS_PER_SHARD
    factor = 1.0 / math.sqrt(HEAD_WIDTH)
    query_pile = query_row_set.reshape(block_list, TOKENS_PER_SHARD, KEY_VALUE_HEADS, GROUP_QUERIES, HEAD_WIDTH)
    key_pile = key_row_set.reshape(block_list, TOKENS_PER_SHARD, KEY_VALUE_HEADS, HEAD_WIDTH)
    value_pile = value_row_set.reshape(block_list, TOKENS_PER_SHARD, KEY_VALUE_HEADS, HEAD_WIDTH)
    gradient_pile = gradient_row_set.reshape(block_list, TOKENS_PER_SHARD, KEY_VALUE_HEADS, GROUP_QUERIES, HEAD_WIDTH)

    def pick(stack, index):
        return lax.dynamic_index_in_dim(stack, jnp.maximum(index, 0).astype(jnp.int32), 0, keepdims=False)
    statistic_init = jnp.zeros((TOKENS_PER_SHARD, KEY_VALUE_HEADS, GROUP_QUERIES), jnp.float32)
    query_gradient_init = jnp.zeros((TOKENS_PER_SHARD, KEY_VALUE_HEADS, GROUP_QUERIES, HEAD_WIDTH), jnp.float32)
    key_gradient_init = jnp.zeros((TOKENS_PER_SHARD, KEY_VALUE_HEADS, HEAD_WIDTH), jnp.float32)

    def forward_block(query_block):
        query = pick(query_pile, query_block)
        grad_out = pick(gradient_pile, query_block)
        row_total = statistic_init
        weighted = query_gradient_init
        for offset in range(REACH):
            key_block = query_block - offset
            visible = pair_mask(doc_lengths, query_block, key_block, TOKENS_PER_SHARD)
            key_part = pick(key_pile, key_block)
            value_part = pick(value_pile, key_block)
            part_total, part_sum = lax.cond(jnp.any(visible), lambda: forward_pair(query, key_part, value_part, visible, factor), lambda: (statistic_init, query_gradient_init))
            row_total = row_total + part_total
            weighted = weighted + part_sum
        output = weighted / row_total[..., None]
        delta = lax.optimization_barrier(jnp.sum(grad_out.astype(jnp.float32) * output, axis=-1))
        return (row_total, delta)
    block_ids = jnp.arange(block_list, dtype=jnp.int32)
    totals, deltas = lax.map(forward_block, block_ids)

    def backward_block(carry, query_block):
        key_gradient_sum, value_gradient_sum = carry
        query = pick(query_pile, query_block)
        grad_out = pick(gradient_pile, query_block)
        row_total = pick(totals, query_block)
        delta = pick(deltas, query_block)
        grad_query = query_gradient_init
        for offset in range(REACH):
            key_block = query_block - offset
            visible = pair_mask(doc_lengths, query_block, key_block, TOKENS_PER_SHARD)
            key_part = pick(key_pile, key_block)
            value_part = pick(value_pile, key_block)
            term_query, term_key, term_value = lax.cond(jnp.any(visible), lambda: backward_pair(query, key_part, value_part, grad_out, visible, row_total, delta, factor), lambda: (query_gradient_init, key_gradient_init, key_gradient_init))
            grad_query = grad_query + term_query
            target = jnp.maximum(key_block, 0).astype(jnp.int32)
            key_gradient_sum = key_gradient_sum.at[target].add(term_key)
            value_gradient_sum = value_gradient_sum.at[target].add(term_value)
        return ((key_gradient_sum, value_gradient_sum), grad_query.astype(jnp.bfloat16))
    start_position = (jnp.zeros((block_list, TOKENS_PER_SHARD, KEY_VALUE_HEADS, HEAD_WIDTH), jnp.float32), jnp.zeros((block_list, TOKENS_PER_SHARD, KEY_VALUE_HEADS, HEAD_WIDTH), jnp.float32))
    (key_gradient_sum, value_gradient_sum), query_gradient_sum = lax.scan(backward_block, start_position, block_ids)
    row_list = block_list * TOKENS_PER_SHARD
    return (query_gradient_sum.reshape(row_list, QUERY_HEADS * HEAD_WIDTH), key_gradient_sum.astype(jnp.bfloat16).reshape(row_list, KEY_VALUE_HEADS * HEAD_WIDTH), value_gradient_sum.astype(jnp.bfloat16).reshape(row_list, KEY_VALUE_HEADS * HEAD_WIDTH))

def reference(queries, key_state_vectors, value_state_vectors, output_gradient, lengths):
    grad_queries, grad_keys, grad_values = lax.map(lambda parts: one_batch(parts[0], parts[1], parts[2], parts[3], parts[4]), (queries, key_state_vectors, value_state_vectors, output_gradient, lengths))
    return (grad_queries, grad_keys, grad_values)
```

```python
import math

import jax
import jax.numpy as jnp
from jax import lax
from jax.experimental import pallas as pl
from jax.experimental.pallas import tpu as pltpu
from jax.sharding import PartitionSpec as P

HEAD = 128
ROWS = 128
PAIR = 2 * ROWS
GROUP = 8
GROUPS = 2
SIDE = 4
DOCS = 16
SLOTS = 4
FACTOR = 1.0 / math.sqrt(HEAD)
LOG2_FACTOR = FACTOR * math.log2(math.e)
BF16 = jnp.bfloat16
F32 = jnp.float32
NT = (((1,), (1,)), ((), ()))
NN = (((1,), (0,)), ((), ()))


def dot(a, b, dims):
    return lax.dot_general(a, b, dims, preferred_element_type=F32)


def kernel(
    lengths, q_hbm, k_hbm, v_hbm, g_hbm,
    dq_hbm, dk_hbm, dv_hbm,
    q_s, g_s, kv, relay, bias, w_s, dp_s, l_s, d_s, p_s, ds_s, own, out_stage, ret_send, ret, fwd_stage, back,
    dq_s, kt_s,
    q_sem, kv_sem, kv_lsem, y_send, y_recv, x_send, x_recv,
    r_send, r_recv, b_send, b_recv, o_sem, o_send, o_recv, dq_sem, dq_send, dq_recv,
):
    dp_at = lax.axis_index("dp")
    me = lax.axis_index("ctx")
    chip, core = me // 2, me % 2
    px, py = chip // SIDE, chip % SIDE
    other = 1 - core

    def at(x, y, k):
        return {"ctx": (((x + SIDE) % SIDE) * SIDE + (y + SIDE) % SIDE) * 2 + k}

    sibling = at(px, py, other)
    x_next, x_prev = at(px + 1, py, core), at(px - 1, py, core)
    ring = [None] + [at(px, py + j, core) for j in range(1, SIDE)]

    def remote(src, dst, send, recv, where):
        return pltpu.make_async_remote_copy(
            src_ref=src, dst_ref=dst, send_sem=send, recv_sem=recv,
            device_id=where, device_id_type=pl.DeviceIdType.MESH,
        )

    mine = pl.ds(pl.multiple_of(core * ROWS, ROWS), ROWS)
    theirs = pl.ds(pl.multiple_of(other * ROWS, ROWS), ROWS)
    half = GROUPS * GROUP * HEAD
    my_heads = pl.ds(pl.multiple_of(core * half, HEAD), half)
    their_heads = pl.ds(pl.multiple_of(other * half, HEAD), half)

    def group_cols(k, gi):
        return pl.ds(pl.multiple_of((k * GROUPS + gi) * HEAD, HEAD), HEAD)

    local = []
    for gi in range(GROUPS):
        for t, src in enumerate((k_hbm, v_hbm)):
            cp = pltpu.make_async_copy(src.at[:, group_cols(core, gi)], kv.at[gi, 0, t, mine], kv_lsem.at[gi, t])
            cp.start()
            local.append(cp)
    q_local = []
    for t, (src, dst) in enumerate(((q_hbm, q_s), (g_hbm, g_s))):
        cp = pltpu.make_async_copy(src.at[:, my_heads], dst.at[mine], q_sem.at[2, t])
        cp.start()
        q_local.append(cp)

    barrier = pltpu.get_barrier_semaphore()
    for peer in [sibling, x_next, x_prev] + ring[1:]:
        pl.semaphore_signal(barrier, inc=1, device_id=peer, device_id_type=pl.DeviceIdType.MESH)
    pl.semaphore_wait(barrier, 6)

    kv_swap = []
    for gi in range(GROUPS):
        for t, src in enumerate((k_hbm, v_hbm)):
            cp = remote(
                src.at[:, group_cols(other, gi)], kv.at[gi, 0, t, mine], kv_sem.at[0, gi, t], kv_sem.at[1, gi, t], sibling
            )
            cp.start()
            kv_swap.append(cp)
    q_swap = []
    for t, (src, dst) in enumerate(((q_hbm, q_s), (g_hbm, g_s))):
        cp = remote(src.at[:, their_heads], dst.at[mine], q_sem.at[0, t], q_sem.at[1, t], sibling)
        cp.start()
        q_swap.append(cp)

    def x_copy(gi):
        return remote(kv.at[gi, 0], relay.at[gi], x_send.at[gi], x_recv.at[gi], x_next)

    def y_copy(gi, j, src):
        return remote(src, kv.at[gi, j], y_send.at[gi, j], y_recv.at[gi, j], ring[j])

    for gi in range(GROUPS):
        for t in range(2):
            local[2 * gi + t].wait()
            kv_swap[2 * gi + t].wait_recv()

        @pl.when(py > 0)
        def _():
            x_copy(gi).start()

        for j in range(1, SLOTS):

            @pl.when(py + j < SIDE)
            def _():
                y_copy(gi, j, kv.at[gi, 0]).start()

    q_pos = chip * PAIR + lax.broadcasted_iota(jnp.int32, (8, PAIR), 1)
    start = jnp.zeros((8, PAIR), jnp.int32)
    bound = jnp.int32(0)
    for d in range(DOCS):
        bound = bound + lengths[dp_at, d]
        start = jnp.where(bound <= q_pos, jnp.maximum(start, bound), start)
    start, q_pos = start[:1], q_pos[:1]
    for j in range(SLOTS):
        k_pos = (chip - j) * PAIR + lax.broadcasted_iota(jnp.int32, (PAIR, PAIR), 0)
        bias[j] = jnp.where((k_pos >= start) & (k_pos <= q_pos), 0.0, -1e30)

    for gi in range(GROUPS):

        @pl.when(py > 0)
        def _():
            x_copy(gi).wait_recv()

        for j in range(1, SLOTS):

            @pl.when(py + j >= SIDE)
            def _():
                y_copy(gi, j, relay.at[gi]).start()

    for t in range(2):
        q_local[t].wait()
        q_swap[t].wait_recv()

    def head_cols(gi, e):
        return pl.ds(pl.multiple_of((gi * GROUP + e) * HEAD, HEAD), HEAD)

    def wide(e):
        return pl.ds(pl.multiple_of(e * PAIR, PAIR), PAIR)

    def ret_copy(gi, j):
        return remote(ret_send.at[gi, j], ret.at[gi, j], r_send.at[gi, j], r_recv.at[gi, j], at(px, py - j, core))

    def back_copy(gi):
        return remote(fwd_stage.at[gi], back.at[gi], b_send.at[gi], b_recv.at[gi], x_prev)

    for gi in range(GROUPS):
        for j in range(SLOTS):
            if j:
                y_copy(gi, j, kv.at[gi, 0]).wait_recv()

            def first(e, _):
                cols = head_cols(gi, e)
                s = dot(kv[gi, j, 0], q_s[:, cols], NT)
                w = jnp.exp2(s * LOG2_FACTOR + bias[j])
                dp = dot(kv[gi, j, 1], g_s[:, cols], NT)
                l = w.reshape(PAIR // 8, 8, PAIR).sum(0)
                d = (w * dp).reshape(PAIR // 8, 8, PAIR).sum(0)
                if j:
                    l_s[e] += l
                    d_s[e] += d
                else:
                    l_s[e] = l
                    d_s[e] = d
                w_s[j, e] = w
                dp_s[j, e] = dp
                return 0

            lax.fori_loop(0, GROUP, first, 0, unroll=2)
            kt_s[:, j * PAIR : (j + 1) * PAIR] = kv[gi, j, 0].T

        def stats(e, _):
            r = 1.0 / l_s[e].sum(0, keepdims=True)
            d = d_s[e].sum(0, keepdims=True) * r
            l_s[e] = jnp.broadcast_to(r, (8, PAIR))
            d_s[e] = jnp.broadcast_to(d, (8, PAIR))
            return 0

        lax.fori_loop(0, GROUP, stats, 0, unroll=True)

        for j in (3, 2, 1, 0):
            dk = jnp.zeros((PAIR, HEAD), F32)
            dv = jnp.zeros((PAIR, HEAD), F32)
            for e in range(GROUP):
                cols = head_cols(gi, e)
                p = w_s[j, e] * l_s[e, :1]
                ds = (p * (dp_s[j, e] - d_s[e, :1])).astype(BF16)
                ds_s[e, j * PAIR : (j + 1) * PAIR] = ds
                dv = dv + dot(p.astype(BF16), g_s[:, cols], NN)
                dk = dk + dot(ds, q_s[:, cols], NN)
            if j:
                ret_send[gi, j, 0] = dk.astype(BF16)
                ret_send[gi, j, 1] = dv.astype(BF16)
                ret_copy(gi, j).start()
            else:
                own[gi, 0] = dk
                own[gi, 1] = dv

        def last(e, _):
            dqt = dot(kt_s[...], ds_s[e], NN) * FACTOR
            dq_s[:, head_cols(gi, e)] = dqt.astype(BF16).T
            return 0

        lax.fori_loop(0, GROUP, last, 0, unroll=2)

    dq_local = pltpu.make_async_copy(dq_s.at[mine], dq_hbm.at[:, my_heads], dq_sem)
    dq_swap = remote(dq_s.at[theirs], dq_hbm.at[:, my_heads], dq_send, dq_recv, sibling)
    dq_local.start()
    dq_swap.start()

    outs = []
    for gi in range(GROUPS):
        for j in range(1, SLOTS):
            ret_copy(gi, j).wait_recv()

        @pl.when(py > 0)
        def _():
            total = jnp.zeros((2, PAIR, HEAD), F32)
            for j in range(1, SLOTS):
                total = total + jnp.where(py + j >= SIDE, ret[gi, j].astype(F32), 0.0)
            fwd_stage[gi] = total.astype(BF16)
            back_copy(gi).start()

    for gi in range(GROUPS):
        total = own[gi]
        for j in range(1, SLOTS):
            total = total + jnp.where(py + j < SIDE, ret[gi, j].astype(F32), 0.0)
        own[gi] = total

        @pl.when(py > 0)
        def _():
            back_copy(gi).wait_recv()
            own[gi] += back[gi].astype(F32)

        out_stage[gi, 0] = (own[gi, 0] * FACTOR).astype(BF16)
        out_stage[gi, 1] = own[gi, 1].astype(BF16)
        for t, dst in enumerate((dk_hbm, dv_hbm)):
            cols = group_cols(core, gi)
            keep = pltpu.make_async_copy(out_stage.at[gi, t, mine], dst.at[:, cols], o_sem.at[gi, t])
            give = remote(out_stage.at[gi, t, theirs], dst.at[:, cols], o_send.at[gi, t], o_recv.at[gi, t], sibling)
            keep.start()
            give.start()
            outs.append((keep, give))

    for keep, give in outs:
        keep.wait()
        give.wait()
    dq_local.wait()
    dq_swap.wait()
    for cp in kv_swap + q_swap:
        cp.wait_send()
    for gi in range(GROUPS):
        for j in range(1, SLOTS):
            y_copy(gi, j, kv.at[gi, 0]).wait_send()
            ret_copy(gi, j).wait_send()

        @pl.when(py > 0)
        def _():
            x_copy(gi).wait_send()
            back_copy(gi).wait_send()


def shards(queries, keys, values, grads, lengths):
    q, k, v, g = queries[0], keys[0], values[0], grads[0]
    vmem = pltpu.VMEM
    dma = pltpu.SemaphoreType.DMA
    hbm = pl.BlockSpec(memory_space=pl.ANY)
    dq, dk, dv = pl.pallas_call(
        kernel,
        out_shape=[jax.ShapeDtypeStruct(a.shape, BF16) for a in (q, k, v)],
        in_specs=[pl.BlockSpec(memory_space=pltpu.SMEM)] + [hbm] * 4,
        out_specs=[hbm] * 3,
        scratch_shapes=[
            vmem((PAIR, GROUPS * GROUP * HEAD), BF16),
            vmem((PAIR, GROUPS * GROUP * HEAD), BF16),
            vmem((GROUPS, SLOTS, 2, PAIR, HEAD), BF16),
            vmem((GROUPS, 2, PAIR, HEAD), BF16),
            vmem((SLOTS, PAIR, PAIR), F32),
            vmem((SLOTS, GROUP, PAIR, PAIR), F32),
            vmem((SLOTS, GROUP, PAIR, PAIR), F32),
            vmem((GROUP, 8, PAIR), F32),
            vmem((GROUP, 8, PAIR), F32),
            vmem((8, 128), F32),
            vmem((GROUP, SLOTS * PAIR, PAIR), BF16),
            vmem((GROUPS, 2, PAIR, HEAD), F32),
            vmem((GROUPS, 2, PAIR, HEAD), BF16),
            vmem((GROUPS, SLOTS, 2, PAIR, HEAD), BF16),
            vmem((GROUPS, SLOTS, 2, PAIR, HEAD), BF16),
            vmem((GROUPS, 2, PAIR, HEAD), BF16),
            vmem((GROUPS, 2, PAIR, HEAD), BF16),
            vmem((PAIR, GROUPS * GROUP * HEAD), BF16),
            vmem((HEAD, SLOTS * PAIR), BF16),
            dma((3, 2)),
            dma((2, GROUPS, 2)),
            dma((GROUPS, 2)),
            dma((GROUPS, SLOTS)), dma((GROUPS, SLOTS)),
            dma((GROUPS,)), dma((GROUPS,)),
            dma((GROUPS, SLOTS)), dma((GROUPS, SLOTS)),
            dma((GROUPS,)), dma((GROUPS,)),
            dma((GROUPS, 2)), dma((GROUPS, 2)), dma((GROUPS, 2)),
            dma, dma, dma,
        ],
        compiler_params=pltpu.CompilerParams(
            collective_id=0, has_side_effects=True, vmem_limit_bytes=56 << 20
        ),
    )(lengths, q, k, v, g)
    return dq[None], dk[None], dv[None]


def solution(mesh):
    spec = P("dp", "ctx", None)
    return jax.shard_map(
        shards,
        mesh=mesh,
        in_specs=(spec, spec, spec, spec, P()),
        out_specs=(spec, spec, spec),
        check_vma=False,
    )
```

```python
import math

import jax
import jax.numpy as jnp
from jax import lax
from jax.experimental import pallas as pl
from jax.experimental.pallas import tpu as pltpu
from jax.sharding import PartitionSpec as P

HEAD = 128
ROWS = 128
PAIR = 2 * ROWS
GROUP = 8
GROUPS = 2
SIDE = 4
DOCS = 16
SLOTS = 4
FACTOR = 1.0 / math.sqrt(HEAD)
LOG2_FACTOR = FACTOR * math.log2(math.e)
BF16 = jnp.bfloat16
F32 = jnp.float32
NT = (((1,), (1,)), ((), ()))
NN = (((1,), (0,)), ((), ()))


def dot(a, b, dims):
    return lax.dot_general(a, b, dims, preferred_element_type=F32)


def kernel(
    lengths, q_hbm, k_hbm, v_hbm, g_hbm,
    dq_hbm, dk_hbm, dv_hbm,
    q_s, g_s, stage, kv, bias, w_s, dp_s, l_s, d_s, ds_s, ret_send, ret, own, own_rx, out_s, dq_s, kt_s,
    ql_sem, q_send, q_recv, st_sem, own_sem, kv_send, kv_recv, f_send, r_send, r_recv, b_send, o_send, o_recv,
    out_sem, dq_sem, dq_send, dq_recv,
):
    dp_at = lax.axis_index("dp")
    me = lax.axis_index("ctx")
    chip, core = me // 2, me % 2
    py = chip % SIDE
    other = 1 - core
    chips = SIDE * SIDE

    def at(c, k):
        return {"ctx": ((c + chips) % chips) * 2 + k}

    sibling = at(chip, other)

    def remote(src, dst, send, recv, where):
        return pltpu.make_async_remote_copy(
            src_ref=src, dst_ref=dst, send_sem=send, recv_sem=recv,
            device_id=where, device_id_type=pl.DeviceIdType.MESH,
        )

    def rows_of(k):
        return pl.ds(pl.multiple_of(k * ROWS, ROWS), ROWS)

    mine, theirs = rows_of(core), rows_of(other)
    half = GROUPS * GROUP * HEAD
    my_heads = pl.ds(pl.multiple_of(core * half, HEAD), half)

    def group_cols(k, gi):
        return pl.ds(pl.multiple_of((k * GROUPS + gi) * HEAD, HEAD), HEAD)

    def query_cols(k, gi):
        return pl.ds(pl.multiple_of((k * GROUPS + gi) * GROUP * HEAD, HEAD), GROUP * HEAD)

    staged = []
    for gi in range(GROUPS):
        for h in range(2):
            for t, src in enumerate((k_hbm, v_hbm)):
                cp = pltpu.make_async_copy(src.at[:, group_cols(h, gi)], stage.at[h, gi, t], st_sem.at[h, gi, t])
                cp.start()
                staged.append(cp)
    owned = []
    for gi in range(GROUPS):
        for t, src in enumerate((k_hbm, v_hbm)):
            cp = pltpu.make_async_copy(src.at[:, group_cols(core, gi)], kv.at[gi, 0, t, mine], own_sem.at[gi, t])
            cp.start()
            owned.append(cp)
    q_local = []
    for gi in range(GROUPS):
        for t, (src, dst) in enumerate(((q_hbm, q_s), (g_hbm, g_s))):
            cp = pltpu.make_async_copy(src.at[:, query_cols(core, gi)], dst.at[gi, mine], ql_sem.at[gi, t])
            cp.start()
            q_local.append(cp)

    barrier = pltpu.get_barrier_semaphore()
    peers = [sibling] + [at(chip + d, k) for j in range(1, SLOTS) for d in (j, -j) for k in range(2)]
    peers += [at(chip + SIDE, core), at(chip - SIDE, core)]
    for peer in peers:
        pl.semaphore_signal(barrier, inc=1, device_id=peer, device_id_type=pl.DeviceIdType.MESH)
    pl.semaphore_wait(barrier, len(peers))
    for cp in staged:
        cp.wait()

    def kv_copy(gi, j, h):
        if j == 1:
            wraps = py == SIDE - 1
            to, slot = jnp.where(wraps, chip - (SIDE - 1), chip + 1), jnp.where(wraps, SLOTS, 1)
        else:
            to, slot = chip + j, j
        return remote(
            stage.at[h, gi], kv.at[gi, slot, :, mine], kv_send.at[gi, j, h], kv_recv.at[gi, slot, core], at(to, h)
        )

    def kv_swap(gi):
        return remote(
            stage.at[other, gi], kv.at[gi, 0, :, mine], kv_send.at[gi, 0, 0], kv_recv.at[gi, 0, core], sibling
        )

    def kv_arrived(gi, slot, k):
        return remote(stage.at[0, gi], kv.at[gi, slot, :, rows_of(k)], kv_send.at[gi, 0, 0], kv_recv.at[gi, slot, k], sibling)

    def kv_forward(gi, k):
        return remote(
            kv.at[gi, SLOTS, :, rows_of(k)], kv.at[gi, 1, :, rows_of(k)], f_send.at[gi, k], kv_recv.at[gi, 1, k],
            at(chip + SIDE, core),
        )

    def q_swap(gi, t):
        src, dst = ((q_hbm, q_s), (g_hbm, g_s))[t]
        return remote(src.at[:, query_cols(other, gi)], dst.at[gi, mine], q_send.at[gi, t], q_recv.at[gi, t], sibling)

    def send_kv(gi):
        kv_swap(gi).start()
        for j in range(1, SLOTS):
            for h in range(2):
                kv_copy(gi, j, h).start()

    def forward_kv(gi):
        @pl.when(py == 0)
        def _():
            for k in range(2):
                kv_arrived(gi, SLOTS, k).wait_recv()
                kv_forward(gi, k).start()

    send_kv(0)
    for t in range(2):
        q_swap(0, t).start()
    send_kv(1)
    for t in range(2):
        q_swap(1, t).start()

    q_pos = chip * PAIR + lax.broadcasted_iota(jnp.int32, (8, PAIR), 1)
    start = jnp.zeros((8, PAIR), jnp.int32)
    bound = jnp.int32(0)
    for d in range(DOCS):
        bound = bound + lengths[dp_at, d]
        start = jnp.where(bound <= q_pos, jnp.maximum(start, bound), start)
    start, q_pos = start[:1], q_pos[:1]
    for j in range(SLOTS):
        k_pos = (chip - j) * PAIR + lax.broadcasted_iota(jnp.int32, (PAIR, PAIR), 0)
        bias[j] = jnp.where((k_pos >= start) & (k_pos <= q_pos), 0.0, -1e30)

    def head_cols(e):
        return pl.ds(pl.multiple_of(e * HEAD, HEAD), HEAD)

    def weights(gi, j):
        if j:
            for k in range(2):
                kv_arrived(gi, j, k).wait_recv()
        else:
            for t in range(2):
                owned[2 * gi + t].wait()
                q_local[2 * gi + t].wait()
                q_swap(gi, t).wait_recv()
            kv_arrived(gi, 0, other).wait_recv()

        def first(e, _):
            cols = head_cols(e)
            s = dot(kv[gi, j, 0], q_s[gi, :, cols], NT)
            w = jnp.exp2(s * LOG2_FACTOR + bias[j])
            dp = dot(kv[gi, j, 1], g_s[gi, :, cols], NT)
            l = w.reshape(PAIR // 8, 8, PAIR).sum(0)
            d = (w * dp).reshape(PAIR // 8, 8, PAIR).sum(0)
            if j:
                l_s[gi, e] += l
                d_s[gi, e] += d
            else:
                l_s[gi, e] = l
                d_s[gi, e] = d
            w_s[gi, j, e] = w
            dp_s[gi, j, e] = dp
            return 0

        lax.fori_loop(0, GROUP, first, 0, unroll=2)
        kt_s[gi, :, j * PAIR : (j + 1) * PAIR] = kv[gi, j, 0].T

    def stats(gi):
        for e in range(GROUP):
            r = 1.0 / l_s[gi, e].sum(0, keepdims=True)
            d = d_s[gi, e].sum(0, keepdims=True) * r
            l_s[gi, e] = jnp.broadcast_to(r, (8, PAIR))
            d_s[gi, e] = jnp.broadcast_to(d, (8, PAIR))

    def ret_copy(gi, j, k):
        if j == 1:
            wraps = py == 0
            to, slot = jnp.where(wraps, chip + SIDE - 1, chip - 1), jnp.where(wraps, SLOTS, 1)
        else:
            to, slot = chip - j, j
        return remote(ret_send.at[gi, j, k], ret.at[core, gi, slot], r_send.at[gi, j, k], r_recv.at[core, gi, slot], at(to, k))

    def ret_arrived(h, gi, slot):
        return remote(ret_send.at[gi, 1, 0], ret.at[h, gi, slot], r_send.at[gi, 1, 0], r_recv.at[h, gi, slot], sibling)

    def ret_forward(gi, h):
        return remote(ret.at[h, gi, SLOTS], ret.at[h, gi, 1], b_send.at[gi, h], r_recv.at[h, gi, 1], at(chip - SIDE, core))

    def forward_ret(gi):
        @pl.when(py == SIDE - 1)
        def _():
            for h in range(2):
                ret_arrived(h, gi, SLOTS).wait_recv()
                ret_forward(gi, h).start()

    def own_swap(gi):
        return remote(own.at[gi, :, theirs], own_rx.at[gi], o_send.at[gi], o_recv.at[gi], sibling)

    def terms(gi, j):
        dk = jnp.zeros((PAIR, HEAD), F32)
        dv = jnp.zeros((PAIR, HEAD), F32)
        for e in range(GROUP):
            cols = head_cols(e)
            p = w_s[gi, j, e] * l_s[gi, e, :1]
            ds = (p * (dp_s[gi, j, e] - d_s[gi, e, :1])).astype(BF16)
            ds_s[e, j * PAIR : (j + 1) * PAIR] = ds
            dv = dv + dot(p.astype(BF16), g_s[gi, :, cols], NN)
            dk = dk + dot(ds, q_s[gi, :, cols], NN)
        if j:
            for t, total in enumerate((dk, dv)):
                low = total.astype(BF16)
                for k in range(2):
                    ret_send[gi, j, k, t] = low[k * ROWS : (k + 1) * ROWS]
            for k in range(2):
                ret_copy(gi, j, k).start()
        else:
            own[gi, 0] = dk
            own[gi, 1] = dv
            own_swap(gi).start()

    def dq_local(gi):
        return pltpu.make_async_copy(dq_s.at[gi, mine], dq_hbm.at[:, query_cols(core, gi)], dq_sem.at[gi])

    def dq_swap(gi):
        return remote(dq_s.at[gi, theirs], dq_hbm.at[:, query_cols(core, gi)], dq_send.at[gi], dq_recv.at[gi], sibling)

    def query_grads(gi):
        def last(e, _):
            dqt = dot(kt_s[gi], ds_s[e], NN) * FACTOR
            dq_s[gi, :, head_cols(e)] = dqt.astype(BF16).T
            return 0

        lax.fori_loop(0, GROUP, last, 0, unroll=2)
        dq_local(gi).start()
        dq_swap(gi).start()

    weights(0, 0)
    forward_kv(0)
    weights(1, 0)
    for j in range(1, SLOTS):
        weights(0, j)
    forward_kv(1)
    stats(0)
    for j in (1, 3, 2, 0):
        terms(0, j)
    query_grads(0)
    for j in range(1, SLOTS):
        weights(1, j)
    forward_ret(0)
    stats(1)
    for j in (1, 3, 2, 0):
        terms(1, j)
    forward_ret(1)
    query_grads(1)

    for gi in range(GROUPS):
        for h, mine_too in ((core, True), (other, False)):
            if mine_too:
                total = own[gi, :, mine]
            else:
                own_swap(gi).wait_recv()
                total = own_rx[gi]
            for j in range(1, SLOTS):
                ret_arrived(h, gi, j).wait_recv()
                total = total + ret[h, gi, j].astype(F32)
            out_s[0, :, group_cols(h, gi)] = (total[0] * FACTOR).astype(BF16)
            out_s[1, :, group_cols(h, gi)] = total[1].astype(BF16)
    outs = []
    for t, dst in enumerate((dk_hbm, dv_hbm)):
        cp = pltpu.make_async_copy(out_s.at[t], dst, out_sem.at[t])
        cp.start()
        outs.append(cp)
    for cp in outs:
        cp.wait()
    for gi in range(GROUPS):
        dq_local(gi).wait()
        dq_swap(gi).wait()
        kv_swap(gi).wait_send()
        own_swap(gi).wait_send()
        for t in range(2):
            q_swap(gi, t).wait_send()
        for j in range(1, SLOTS):
            for k in range(2):
                kv_copy(gi, j, k).wait_send()
                ret_copy(gi, j, k).wait_send()

        @pl.when(py == 0)
        def _():
            for k in range(2):
                kv_forward(gi, k).wait_send()

        @pl.when(py == SIDE - 1)
        def _():
            for h in range(2):
                ret_forward(gi, h).wait_send()


def handed_on(dq, dk, dv, dq_out, dk_out, dv_out):
    dq_out[...] = dq[...]
    dk_out[...] = dk[...]
    dv_out[...] = dv[...]


def shards(queries, keys, values, grads, lengths):
    q, k, v, g = queries[0], keys[0], values[0], grads[0]
    vmem = pltpu.VMEM
    dma = pltpu.SemaphoreType.DMA
    hbm = pl.BlockSpec(memory_space=pl.ANY)
    dq, dk, dv = pl.pallas_call(
        kernel,
        out_shape=[jax.ShapeDtypeStruct(a.shape, BF16) for a in (q, k, v)],
        in_specs=[pl.BlockSpec(memory_space=pltpu.SMEM)] + [hbm] * 4,
        out_specs=[hbm] * 3,
        scratch_shapes=[
            vmem((GROUPS, PAIR, GROUP * HEAD), BF16),
            vmem((GROUPS, PAIR, GROUP * HEAD), BF16),
            vmem((2, GROUPS, 2, ROWS, HEAD), BF16),
            vmem((GROUPS, SLOTS + 1, 2, PAIR, HEAD), BF16),
            vmem((SLOTS, PAIR, PAIR), F32),
            vmem((GROUPS, SLOTS, GROUP, PAIR, PAIR), F32),
            vmem((GROUPS, SLOTS, GROUP, PAIR, PAIR), F32),
            vmem((GROUPS, GROUP, 8, PAIR), F32),
            vmem((GROUPS, GROUP, 8, PAIR), F32),
            vmem((GROUP, SLOTS * PAIR, PAIR), BF16),
            vmem((GROUPS, SLOTS, 2, 2, ROWS, HEAD), BF16),
            vmem((2, GROUPS, SLOTS + 1, 2, ROWS, HEAD), BF16),
            vmem((GROUPS, 2, PAIR, HEAD), F32),
            vmem((GROUPS, 2, ROWS, HEAD), F32),
            vmem((2, ROWS, 2 * GROUPS * HEAD), BF16),
            vmem((GROUPS, PAIR, GROUP * HEAD), BF16),
            vmem((GROUPS, HEAD, SLOTS * PAIR), BF16),
            dma((GROUPS, 2)), dma((GROUPS, 2)), dma((GROUPS, 2)),
            dma((2, GROUPS, 2)), dma((GROUPS, 2)),
            dma((GROUPS, SLOTS, 2)), dma((GROUPS, SLOTS + 1, 2)), dma((GROUPS, 2)),
            dma((GROUPS, SLOTS, 2)), dma((2, GROUPS, SLOTS + 1)), dma((GROUPS, 2)),
            dma((GROUPS,)), dma((GROUPS,)),
            dma((2,)), dma((GROUPS,)), dma((GROUPS,)), dma((GROUPS,)),
        ],
        compiler_params=pltpu.CompilerParams(
            collective_id=0, has_side_effects=True, vmem_limit_bytes=60 << 20
        ),
    )(lengths, q, k, v, g)
    steps = 4
    specs = [pl.BlockSpec((ROWS // steps, a.shape[1]), lambda i: (i, 0)) for a in (q, k, v)]
    dq, dk, dv = pl.pallas_call(
        handed_on, grid=(steps,), out_shape=[jax.ShapeDtypeStruct(a.shape, BF16) for a in (q, k, v)],
        in_specs=specs, out_specs=specs,
    )(dq, dk, dv)
    return dq[None], dk[None], dv[None]


def solution(mesh):
    spec = P("dp", "ctx", None)
    return jax.shard_map(
        shards,
        mesh=mesh,
        in_specs=(spec, spec, spec, spec, P()),
        out_specs=(spec, spec, spec),
        check_vma=False,
    )
```

```python
import math

import jax
import jax.numpy as jnp
from jax import lax
from jax.experimental import pallas as pl
from jax.experimental.pallas import tpu as pltpu
from jax.sharding import PartitionSpec as P

HEAD = 128
ROWS = 128
PAIR = 2 * ROWS
GROUP = 8
GROUPS = 2
SIDE = 4
DOCS = 16
SLOTS = 4
FACTOR = 1.0 / math.sqrt(HEAD)
LOG2_FACTOR = FACTOR * math.log2(math.e)
BF16 = jnp.bfloat16
F32 = jnp.float32
NN = (((1,), (0,)), ((), ()))


def dot(a, b, dims):
    return lax.dot_general(a, b, dims, preferred_element_type=F32)


def kernel(
    lengths, q_hbm, k_hbm, v_hbm, g_hbm,
    dq_hbm, dk_hbm, dv_hbm,
    q_s, g_s, qt_s, gt_s, qh_s, gh_s, stage, kv, bias, w_s, dp_s, l_s, d_s, ds_s, ex_send, ex, held, ret_send, ret, own, own_rx, out_s, dq_s, kt_s,
    ql_sem, q_send, q_recv, st_sem, own_sem, kv_send, kv_recv, f_send, h_send, e_send, e_recv, r_send, r_recv, b_send, o_send, o_recv,
    out_sem, dq_sem, dq_send, dq_recv,
):
    dp_at = lax.axis_index("dp")
    me = lax.axis_index("ctx")
    chip, core = me // 2, me % 2
    py = chip % SIDE
    other = 1 - core
    chips = SIDE * SIDE

    def at(c, k):
        return {"ctx": ((c + chips) % chips) * 2 + k}

    sibling = at(chip, other)

    def remote(src, dst, send, recv, where):
        return pltpu.make_async_remote_copy(
            src_ref=src, dst_ref=dst, send_sem=send, recv_sem=recv,
            device_id=where, device_id_type=pl.DeviceIdType.MESH,
        )

    def rows_of(k):
        return pl.ds(pl.multiple_of(k * ROWS, ROWS), ROWS)

    mine, theirs = rows_of(core), rows_of(other)
    half = GROUPS * GROUP * HEAD
    my_heads = pl.ds(pl.multiple_of(core * half, HEAD), half)

    def group_cols(k, gi):
        return pl.ds(pl.multiple_of((k * GROUPS + gi) * HEAD, HEAD), HEAD)

    def query_cols(k, gi):
        return pl.ds(pl.multiple_of((k * GROUPS + gi) * GROUP * HEAD, HEAD), GROUP * HEAD)

    staged = []
    for gi in range(GROUPS):
        for h in range(2):
            for t, src in enumerate((k_hbm, v_hbm)):
                cp = pltpu.make_async_copy(src.at[:, group_cols(h, gi)], stage.at[h, gi, t], st_sem.at[h, gi, t])
                cp.start()
                staged.append(cp)
    owned = []
    for gi in range(GROUPS):
        for t, src in enumerate((k_hbm, v_hbm)):
            cp = pltpu.make_async_copy(src.at[:, group_cols(core, gi)], kv.at[gi, 0, t, mine], own_sem.at[gi, t])
            cp.start()
            owned.append(cp)
    q_local = []
    for gi in range(GROUPS):
        for t, (src, dst) in enumerate(((q_hbm, q_s), (g_hbm, g_s))):
            cp = pltpu.make_async_copy(src.at[:, query_cols(core, gi)], dst.at[gi, mine], ql_sem.at[gi, t])
            cp.start()
            q_local.append(cp)

    barrier = pltpu.get_barrier_semaphore()
    peers = [sibling] + [at(chip + d, k) for d in (1, -1, 3, -3) for k in range(2)]
    peers += [at(chip + SIDE, core), at(chip - SIDE, core)]
    for peer in peers:
        pl.semaphore_signal(barrier, inc=1, device_id=peer, device_id_type=pl.DeviceIdType.MESH)
    pl.semaphore_wait(barrier, len(peers))
    for cp in staged:
        cp.wait()

    def kv_copy(gi, j, h, t):
        if j == 1:
            wraps = py == SIDE - 1
            to, slot = jnp.where(wraps, chip - (SIDE - 1), chip + 1), jnp.where(wraps, SLOTS, 1)
        else:
            to, slot = chip + j, j
        return remote(
            stage.at[h, gi, t], kv.at[gi, slot, t, mine], kv_send.at[gi, j, h, t], kv_recv.at[gi, slot, t, core], at(to, h)
        )

    def kv_swap(gi, t):
        return remote(
            stage.at[other, gi, t], kv.at[gi, 0, t, mine], kv_send.at[gi, 0, 0, t], kv_recv.at[gi, 0, t, core], sibling
        )

    def kv_arrived(gi, slot, t, k):
        return remote(
            stage.at[0, gi, t], kv.at[gi, slot, t, rows_of(k)], kv_send.at[gi, 0, 0, t], kv_recv.at[gi, slot, t, k], sibling
        )

    def kv_forward(gi, t, k):
        return remote(
            kv.at[gi, SLOTS, t, rows_of(k)], kv.at[gi, 1, t, rows_of(k)], f_send.at[gi, t, k], kv_recv.at[gi, 1, t, k],
            at(chip + SIDE, core),
        )

    def kv_hop(gi, t):
        slot, to = (1, chip + 1) if t == 0 else (3, chip - 1)
        return remote(kv.at[gi, slot, t], kv.at[gi, 2, t], h_send.at[gi, t], kv_recv.at[gi, 2, t, 0], at(to, core))

    def q_swap(gi, t):
        src, dst = ((q_hbm, q_s), (g_hbm, g_s))[t]
        return remote(src.at[:, query_cols(other, gi)], dst.at[gi, mine], q_send.at[gi, t], q_recv.at[gi, t], sibling)

    def send_kv(gi):
        for t in range(2):
            kv_swap(gi, t).start()
        for t, j in ((0, 1), (1, 3), (1, 1), (0, 3)):
            for h in range(2):
                kv_copy(gi, j, h, t).start()

    def forward_kv(gi):
        @pl.when(py == 0)
        def _():
            for t in range(2):
                for k in range(2):
                    kv_arrived(gi, SLOTS, t, k).wait_recv()
                    kv_forward(gi, t, k).start()

    def hop_kv(gi):
        for t, slot in ((1, 3), (0, 1)):
            for k in range(2):
                kv_arrived(gi, slot, t, k).wait_recv()
            kv_hop(gi, t).start()

    send_kv(0)
    for t in range(2):
        q_swap(0, t).start()
    send_kv(1)
    for t in range(2):
        q_swap(1, t).start()

    q_pos = chip * PAIR + lax.broadcasted_iota(jnp.int32, (8, PAIR), 1)
    start = jnp.zeros((8, PAIR), jnp.int32)
    bound = jnp.int32(0)
    for d in range(DOCS):
        bound = bound + lengths[dp_at, d]
        start = jnp.where(bound <= q_pos, jnp.maximum(start, bound), start)
    start, q_pos = start[:1], q_pos[:1]
    for j in range(SLOTS):
        k_pos = (chip - j) * PAIR + lax.broadcasted_iota(jnp.int32, (PAIR, PAIR), 0)
        bias[j] = jnp.where((k_pos >= start) & (k_pos <= q_pos), 0.0, -1e30)

    def head_cols(e):
        return pl.ds(pl.multiple_of(e * HEAD, HEAD), HEAD)

    def weights(gi, j):
        if j == 2:
            for t in range(2):
                kv_hop(gi, t).wait_recv()
        elif j:
            for k in range(2):
                kv_arrived(gi, j, 1 if j == 1 else 0, k).wait_recv()
        else:
            for t in range(2):
                owned[2 * gi + t].wait()
                q_local[2 * gi + t].wait()
                q_swap(gi, t).wait_recv()
                kv_arrived(gi, 0, t, other).wait_recv()
            for e in range(GROUP):
                cols = slice(e * HEAD, (e + 1) * HEAD)
                at_e = slice(e * PAIR, (e + 1) * PAIR)
                for src, flat, turned in ((q_s, qh_s, qt_s), (g_s, gh_s, gt_s)):
                    block = src[gi, :, cols]
                    flat[gi, at_e] = block
                    turned[gi, e] = block.T

        def first(e, _):
            s = dot(kv[gi, j, 0], qt_s[gi, e], NN)
            w = jnp.exp2(s * LOG2_FACTOR + bias[j])
            dp = dot(kv[gi, j, 1], gt_s[gi, e], NN)
            l = w.reshape(PAIR // 8, 8, PAIR).sum(0)
            d = (w * dp).reshape(PAIR // 8, 8, PAIR).sum(0)
            if j:
                l_s[gi, e] += l
                d_s[gi, e] += d
            else:
                l_s[gi, e] = l
                d_s[gi, e] = d
            w_s[gi, j, e] = w
            dp_s[gi, j, e] = dp
            return 0

        lax.fori_loop(0, GROUP, first, 0, unroll=8)
        kt_s[gi, :, j * PAIR : (j + 1) * PAIR] = kv[gi, j, 0].T

    def stats(gi):
        for e in range(GROUP):
            r = 1.0 / l_s[gi, e].sum(0, keepdims=True)
            d = d_s[gi, e].sum(0, keepdims=True) * r
            l_s[gi, e] = jnp.broadcast_to(r, (8, PAIR))
            d_s[gi, e] = jnp.broadcast_to(d, (8, PAIR))

    def ret_copy(gi, j, t, k):
        if j == 1:
            wraps = py == 0
            to, slot = jnp.where(wraps, chip + SIDE - 1, chip - 1), jnp.where(wraps, SLOTS, 1)
        else:
            to, slot = chip - j, j
        return remote(
            ret_send.at[gi, j, t, k], ret.at[core, gi, slot, t], r_send.at[gi, j, t, k], r_recv.at[core, gi, slot, t], at(to, k)
        )

    def ret_arrived(h, gi, slot, t):
        return remote(ret_send.at[gi, 1, t, 0], ret.at[h, gi, slot, t], r_send.at[gi, 1, t, 0], r_recv.at[h, gi, slot, t], sibling)

    def ret_forward(gi, t, h):
        return remote(
            ret.at[h, gi, SLOTS, t], ret.at[h, gi, 1, t], b_send.at[gi, t, h], r_recv.at[h, gi, 1, t], at(chip - SIDE, core)
        )

    def forward_ret(gi):
        @pl.when(py == SIDE - 1)
        def _():
            for t in (1, 0):
                for h in range(2):
                    ret_arrived(h, gi, SLOTS, t).wait_recv()
                    ret_forward(gi, t, h).start()

    def ex_copy(gi, t):
        return remote(ex_send.at[gi, t], ex.at[gi, t], e_send.at[gi, t], e_recv.at[gi, t], at(chip - 1 if t == 0 else chip + 1, core))

    def send_terms(gi, j, t, total):
        low = total.astype(BF16)
        for k in range(2):
            ret_send[gi, j, t, k] = low[k * ROWS : (k + 1) * ROWS]
            ret_copy(gi, j, t, k).start()

    def own_swap(gi):
        return remote(own.at[gi, :, theirs], own_rx.at[gi], o_send.at[gi], o_recv.at[gi], sibling)

    def terms(gi, j):
        rows = slice(j * PAIR, (j + 1) * PAIR)
        dk = dv = None
        for e0 in range(0, GROUP, 2):
            low = []
            for e in range(e0, e0 + 2):
                p = w_s[gi, j, e] * l_s[gi, e, :1]
                ds_s[gi, rows, e * PAIR : (e + 1) * PAIR] = (p * (dp_s[gi, j, e] - d_s[gi, e, :1])).astype(BF16)
                low.append(p.astype(BF16))
            part = slice(e0 * PAIR, (e0 + 2) * PAIR)
            dv_part = dot(jnp.concatenate(low, axis=1), gh_s[gi, part], NN)
            dk_part = dot(ds_s[gi, rows, part], qh_s[gi, part], NN)
            dv = dv_part if dv is None else dv + dv_part
            dk = dk_part if dk is None else dk + dk_part
        return dk, dv

    def all_terms(gi):
        for t, total in enumerate(terms(gi, 2)):
            ex_send[gi, t] = total.astype(BF16)
            ex_copy(gi, t).start()
        held[0], dv = terms(gi, 1)
        send_terms(gi, 1, 1, dv)
        dk, held[1] = terms(gi, 3)
        send_terms(gi, 3, 0, dk)
        for t in range(2):
            ex_copy(gi, t).wait_recv()
            send_terms(gi, (1, 3)[t], t, held[t] + ex[gi, t].astype(F32))
        own[gi, 0], own[gi, 1] = terms(gi, 0)
        own_swap(gi).start()

    def dq_local(gi):
        return pltpu.make_async_copy(dq_s.at[gi, mine], dq_hbm.at[:, query_cols(core, gi)], dq_sem.at[gi])

    def dq_swap(gi):
        return remote(dq_s.at[gi, theirs], dq_hbm.at[:, query_cols(core, gi)], dq_send.at[gi], dq_recv.at[gi], sibling)

    def query_grads(gi):
        def last(e, _):
            dqt = dot(kt_s[gi], ds_s[gi, :, pl.ds(pl.multiple_of(e * PAIR, PAIR), PAIR)], NN) * FACTOR
            dq_s[gi, :, head_cols(e)] = dqt.astype(BF16).T
            return 0

        lax.fori_loop(0, GROUP, last, 0, unroll=8)
        dq_local(gi).start()
        dq_swap(gi).start()

    weights(0, 0)
    forward_kv(0)
    weights(1, 0)
    hop_kv(0)
    forward_kv(1)
    weights(0, 1)
    weights(0, 3)
    hop_kv(1)
    weights(0, 2)
    stats(0)
    all_terms(0)
    for j in (1, 3, 2):
        weights(1, j)
    forward_ret(0)
    stats(1)
    all_terms(1)
    query_grads(0)
    forward_ret(1)
    query_grads(1)

    for gi in range(GROUPS):
        for h, mine_too in ((core, True), (other, False)):
            if mine_too:
                total = own[gi, :, mine]
            else:
                own_swap(gi).wait_recv()
                total = own_rx[gi]
            for j in (3, 1):
                for t in range(2):
                    ret_arrived(h, gi, j, t).wait_recv()
                total = total + ret[h, gi, j].astype(F32)
            out_s[0, :, group_cols(h, gi)] = (total[0] * FACTOR).astype(BF16)
            out_s[1, :, group_cols(h, gi)] = total[1].astype(BF16)
    outs = []
    for t, dst in enumerate((dk_hbm, dv_hbm)):
        cp = pltpu.make_async_copy(out_s.at[t], dst, out_sem.at[t])
        cp.start()
        outs.append(cp)
    for cp in outs:
        cp.wait()
    for gi in range(GROUPS):
        dq_local(gi).wait()
        dq_swap(gi).wait()
        own_swap(gi).wait_send()
        for t in range(2):
            q_swap(gi, t).wait_send()
            kv_swap(gi, t).wait_send()
            kv_hop(gi, t).wait_send()
            ex_copy(gi, t).wait_send()
            for j in (1, 3):
                for k in range(2):
                    kv_copy(gi, j, k, t).wait_send()
                    ret_copy(gi, j, t, k).wait_send()

        @pl.when(py == 0)
        def _():
            for t in range(2):
                for k in range(2):
                    kv_forward(gi, t, k).wait_send()

        @pl.when(py == SIDE - 1)
        def _():
            for t in range(2):
                for h in range(2):
                    ret_forward(gi, t, h).wait_send()


def handed_on(dq, dk, dv, dq_out, dk_out, dv_out):
    dq_out[...] = dq[...]
    dk_out[...] = dk[...]
    dv_out[...] = dv[...]


def shards(queries, keys, values, grads, lengths):
    q, k, v, g = queries[0], keys[0], values[0], grads[0]
    vmem = pltpu.VMEM
    dma = pltpu.SemaphoreType.DMA
    hbm = pl.BlockSpec(memory_space=pl.ANY)
    dq, dk, dv = pl.pallas_call(
        kernel,
        out_shape=[jax.ShapeDtypeStruct(a.shape, BF16) for a in (q, k, v)],
        in_specs=[pl.BlockSpec(memory_space=pltpu.SMEM)] + [hbm] * 4,
        out_specs=[hbm] * 3,
        scratch_shapes=[
            vmem((GROUPS, PAIR, GROUP * HEAD), BF16),
            vmem((GROUPS, PAIR, GROUP * HEAD), BF16),
            vmem((GROUPS, GROUP, HEAD, PAIR), BF16),
            vmem((GROUPS, GROUP, HEAD, PAIR), BF16),
            vmem((GROUPS, GROUP * PAIR, HEAD), BF16),
            vmem((GROUPS, GROUP * PAIR, HEAD), BF16),
            vmem((2, GROUPS, 2, ROWS, HEAD), BF16),
            vmem((GROUPS, SLOTS + 1, 2, PAIR, HEAD), BF16),
            vmem((SLOTS, PAIR, PAIR), F32),
            vmem((GROUPS, SLOTS, GROUP, PAIR, PAIR), F32),
            vmem((GROUPS, SLOTS, GROUP, PAIR, PAIR), F32),
            vmem((GROUPS, GROUP, 8, PAIR), F32),
            vmem((GROUPS, GROUP, 8, PAIR), F32),
            vmem((GROUPS, SLOTS * PAIR, GROUP * PAIR), BF16),
            vmem((GROUPS, 2, PAIR, HEAD), BF16),
            vmem((GROUPS, 2, PAIR, HEAD), BF16),
            vmem((2, PAIR, HEAD), F32),
            vmem((GROUPS, SLOTS, 2, 2, ROWS, HEAD), BF16),
            vmem((2, GROUPS, SLOTS + 1, 2, ROWS, HEAD), BF16),
            vmem((GROUPS, 2, PAIR, HEAD), F32),
            vmem((GROUPS, 2, ROWS, HEAD), F32),
            vmem((2, ROWS, 2 * GROUPS * HEAD), BF16),
            vmem((GROUPS, PAIR, GROUP * HEAD), BF16),
            vmem((GROUPS, HEAD, SLOTS * PAIR), BF16),
            dma((GROUPS, 2)), dma((GROUPS, 2)), dma((GROUPS, 2)),
            dma((2, GROUPS, 2)), dma((GROUPS, 2)),
            dma((GROUPS, SLOTS, 2, 2)), dma((GROUPS, SLOTS + 1, 2, 2)), dma((GROUPS, 2, 2)), dma((GROUPS, 2)),
            dma((GROUPS, 2)), dma((GROUPS, 2)),
            dma((GROUPS, SLOTS, 2, 2)), dma((2, GROUPS, SLOTS + 1, 2)), dma((GROUPS, 2, 2)),
            dma((GROUPS,)), dma((GROUPS,)),
            dma((2,)), dma((GROUPS,)), dma((GROUPS,)), dma((GROUPS,)),
        ],
        compiler_params=pltpu.CompilerParams(
            collective_id=0, has_side_effects=True, vmem_limit_bytes=60 << 20
        ),
    )(lengths, q, k, v, g)
    steps = 2
    specs = [pl.BlockSpec((ROWS // steps, a.shape[1]), lambda i: (i, 0)) for a in (q, k, v)]
    dq, dk, dv = pl.pallas_call(
        handed_on, grid=(steps,), out_shape=[jax.ShapeDtypeStruct(a.shape, BF16) for a in (q, k, v)],
        in_specs=specs, out_specs=specs,
    )(dq, dk, dv)
    return dq[None], dk[None], dv[None]


def solution(mesh):
    spec = P("dp", "ctx", None)
    return jax.shard_map(
        shards,
        mesh=mesh,
        in_specs=(spec, spec, spec, spec, P()),
        out_specs=(spec, spec, spec),
        check_vma=False,
    )
```

```python
import math

import jax
import jax.numpy as jnp
from jax import lax
from jax.experimental import pallas as pl
from jax.experimental.pallas import tpu as pltpu
from jax.sharding import PartitionSpec as P

HEAD = 128
ROWS = 128
PAIR = 2 * ROWS
GROUP = 8
GROUPS = 2
SIDE = 4
DOCS = 16
SLOTS = 4
FACTOR = 1.0 / math.sqrt(HEAD)
LOG2_FACTOR = FACTOR * math.log2(math.e)
KV_HOPS = (0, 1)
TERM_HOPS = (0, 1)
BF16 = jnp.bfloat16
F32 = jnp.float32
NN = (((1,), (0,)), ((), ()))


def dot(a, b, dims):
    return lax.dot_general(a, b, dims, preferred_element_type=F32)


def kernel(
    lengths, q_hbm, k_hbm, v_hbm, g_hbm,
    dq_hbm, dk_hbm, dv_hbm,
    q_s, g_s, qt_s, gt_s, qh_s, gh_s, stage, kv, bias, w_s, dp_s, l_s, d_s, ds_s, ex_send, ex, held, ret_send, ret, own, own_rx, out_s, dq_s, kt_s,
    ql_sem, q_send, q_recv, st_sem, own_sem, kv_send, kv_recv, f_send, h_send, e_send, e_recv, r_send, r_recv, b_send, o_send, o_recv,
    out_sem, dq_sem, dq_send, dq_recv,
):
    dp_at = lax.axis_index("dp")
    me = lax.axis_index("ctx")
    chip, core = me // 2, me % 2
    py = chip % SIDE
    other = 1 - core
    chips = SIDE * SIDE

    def at(c, k):
        return {"ctx": ((c + chips) % chips) * 2 + k}

    sibling = at(chip, other)

    def remote(src, dst, send, recv, where):
        return pltpu.make_async_remote_copy(
            src_ref=src, dst_ref=dst, send_sem=send, recv_sem=recv,
            device_id=where, device_id_type=pl.DeviceIdType.MESH,
        )

    def rows_of(k):
        return pl.ds(pl.multiple_of(k * ROWS, ROWS), ROWS)

    mine, theirs = rows_of(core), rows_of(other)
    half = GROUPS * GROUP * HEAD
    my_heads = pl.ds(pl.multiple_of(core * half, HEAD), half)

    def group_cols(k, gi):
        return pl.ds(pl.multiple_of((k * GROUPS + gi) * HEAD, HEAD), HEAD)

    def query_cols(k, gi):
        return pl.ds(pl.multiple_of((k * GROUPS + gi) * GROUP * HEAD, HEAD), GROUP * HEAD)

    staged = []
    for gi in range(GROUPS):
        for h in range(2):
            for t, src in enumerate((k_hbm, v_hbm)):
                cp = pltpu.make_async_copy(src.at[:, group_cols(h, gi)], stage.at[h, gi, t], st_sem.at[h, gi, t])
                cp.start()
                staged.append(cp)
    owned = []
    for gi in range(GROUPS):
        for t, src in enumerate((k_hbm, v_hbm)):
            cp = pltpu.make_async_copy(src.at[:, group_cols(core, gi)], kv.at[gi, 0, t, mine], own_sem.at[gi, t])
            cp.start()
            owned.append(cp)
    q_local = []
    for gi in range(GROUPS):
        for t, (src, dst) in enumerate(((q_hbm, q_s), (g_hbm, g_s))):
            cp = pltpu.make_async_copy(src.at[:, query_cols(core, gi)], dst.at[gi, mine], ql_sem.at[gi, t])
            cp.start()
            q_local.append(cp)

    barrier = pltpu.get_barrier_semaphore()
    peers = [sibling] + [at(chip + d, k) for d in (1, -1, 3, -3) for k in range(2)]
    peers += [at(chip + SIDE, core), at(chip - SIDE, core)]
    for peer in peers:
        pl.semaphore_signal(barrier, inc=1, device_id=peer, device_id_type=pl.DeviceIdType.MESH)
    pl.semaphore_wait(barrier, len(peers))
    for cp in staged:
        cp.wait()

    def kv_copy(gi, j, h, t):
        if j == 1:
            wraps = py == SIDE - 1
            to, slot = jnp.where(wraps, chip - (SIDE - 1), chip + 1), jnp.where(wraps, SLOTS, 1)
        else:
            to, slot = chip + j, j
        return remote(
            stage.at[h, gi, t], kv.at[gi, slot, t, mine], kv_send.at[gi, j, h, t], kv_recv.at[gi, slot, t, core], at(to, h)
        )

    def kv_swap(gi, t):
        return remote(
            stage.at[other, gi, t], kv.at[gi, 0, t, mine], kv_send.at[gi, 0, 0, t], kv_recv.at[gi, 0, t, core], sibling
        )

    def kv_arrived(gi, slot, t, k):
        return remote(
            stage.at[0, gi, t], kv.at[gi, slot, t, rows_of(k)], kv_send.at[gi, 0, 0, t], kv_recv.at[gi, slot, t, k], sibling
        )

    def kv_forward(gi, t, k):
        return remote(
            kv.at[gi, SLOTS, t, rows_of(k)], kv.at[gi, 1, t, rows_of(k)], f_send.at[gi, t, k], kv_recv.at[gi, 1, t, k],
            at(chip + SIDE, core),
        )

    def kv_hop(gi, t):
        slot, to = (1, chip + 1) if t == 0 else (3, chip - 1)
        return remote(kv.at[gi, slot, t], kv.at[gi, 2, t], h_send.at[gi, t], kv_recv.at[gi, 2, t, 0], at(to, core))

    def q_swap(gi, t):
        src, dst = ((q_hbm, q_s), (g_hbm, g_s))[t]
        return remote(src.at[:, query_cols(other, gi)], dst.at[gi, mine], q_send.at[gi, t], q_recv.at[gi, t], sibling)

    def send_kv(gi):
        for t in range(2):
            kv_swap(gi, t).start()
        for t, j in ((0, 1), (1, 3), (1, 1), (0, 3), (0, 2), (1, 2)):
            if j == 2 and gi in KV_HOPS:
                continue
            for h in range(2):
                kv_copy(gi, j, h, t).start()

    def forward_kv(gi):
        @pl.when(py == 0)
        def _():
            for t in range(2):
                for k in range(2):
                    kv_arrived(gi, SLOTS, t, k).wait_recv()
                    kv_forward(gi, t, k).start()

    def hop_kv(gi):
        for t, slot in ((1, 3), (0, 1)):
            for k in range(2):
                kv_arrived(gi, slot, t, k).wait_recv()
            if gi in KV_HOPS:
                kv_hop(gi, t).start()

    send_kv(0)
    for t in range(2):
        q_swap(0, t).start()
    send_kv(1)
    for t in range(2):
        q_swap(1, t).start()

    q_pos = chip * PAIR + lax.broadcasted_iota(jnp.int32, (8, PAIR), 1)
    start = jnp.zeros((8, PAIR), jnp.int32)
    bound = jnp.int32(0)
    for d in range(DOCS):
        bound = bound + lengths[dp_at, d]
        start = jnp.where(bound <= q_pos, jnp.maximum(start, bound), start)
    start, q_pos = start[:1], q_pos[:1]
    for j in range(SLOTS):
        k_pos = (chip - j) * PAIR + lax.broadcasted_iota(jnp.int32, (PAIR, PAIR), 0)
        bias[j] = jnp.where((k_pos >= start) & (k_pos <= q_pos), 0.0, -1e30)

    def head_cols(e):
        return pl.ds(pl.multiple_of(e * HEAD, HEAD), HEAD)

    def weights(gi, j):
        if j == 2:
            for t in range(2):
                if gi in KV_HOPS:
                    kv_hop(gi, t).wait_recv()
                else:
                    for k in range(2):
                        kv_arrived(gi, 2, t, k).wait_recv()
        elif j:
            for k in range(2):
                kv_arrived(gi, j, 1 if j == 1 else 0, k).wait_recv()
        else:
            for t in range(2):
                owned[2 * gi + t].wait()
                q_local[2 * gi + t].wait()
                q_swap(gi, t).wait_recv()
                kv_arrived(gi, 0, t, other).wait_recv()
            for e in range(GROUP):
                cols = slice(e * HEAD, (e + 1) * HEAD)
                at_e = slice(e * PAIR, (e + 1) * PAIR)
                for src, flat, turned in ((q_s, qh_s, qt_s), (g_s, gh_s, gt_s)):
                    block = src[gi, :, cols]
                    flat[gi, at_e] = block
                    turned[gi, e] = block.T

        def first(e, _):
            s = dot(kv[gi, j, 0], qt_s[gi, e], NN)
            w = jnp.exp2(s * LOG2_FACTOR + bias[j])
            dp = dot(kv[gi, j, 1], gt_s[gi, e], NN)
            l = w.reshape(PAIR // 8, 8, PAIR).sum(0)
            d = (w * dp).reshape(PAIR // 8, 8, PAIR).sum(0)
            if j:
                l_s[gi, e] += l
                d_s[gi, e] += d
            else:
                l_s[gi, e] = l
                d_s[gi, e] = d
            w_s[gi, j, e] = w
            dp_s[gi, j, e] = dp
            return 0

        lax.fori_loop(0, GROUP, first, 0, unroll=8)
        kt_s[gi, :, j * PAIR : (j + 1) * PAIR] = kv[gi, j, 0].T

    def stats(gi):
        for e in range(GROUP):
            r = 1.0 / l_s[gi, e].sum(0, keepdims=True)
            d = d_s[gi, e].sum(0, keepdims=True) * r
            l_s[gi, e] = jnp.broadcast_to(r, (8, PAIR))
            d_s[gi, e] = jnp.broadcast_to(d, (8, PAIR))

    def ret_copy(gi, j, t, k):
        if j == 1:
            wraps = py == 0
            to, slot = jnp.where(wraps, chip + SIDE - 1, chip - 1), jnp.where(wraps, SLOTS, 1)
        else:
            to, slot = chip - j, j
        return remote(
            ret_send.at[gi, j, t, k], ret.at[core, gi, slot, t], r_send.at[gi, j, t, k], r_recv.at[core, gi, slot, t], at(to, k)
        )

    def ret_arrived(h, gi, slot, t):
        return remote(ret_send.at[gi, 1, t, 0], ret.at[h, gi, slot, t], r_send.at[gi, 1, t, 0], r_recv.at[h, gi, slot, t], sibling)

    def ret_forward(gi, t, h):
        return remote(
            ret.at[h, gi, SLOTS, t], ret.at[h, gi, 1, t], b_send.at[gi, t, h], r_recv.at[h, gi, 1, t], at(chip - SIDE, core)
        )

    def forward_ret(gi):
        @pl.when(py == SIDE - 1)
        def _():
            for t in (1, 0):
                for h in range(2):
                    ret_arrived(h, gi, SLOTS, t).wait_recv()
                    ret_forward(gi, t, h).start()

    def ex_copy(gi, t):
        return remote(ex_send.at[gi, t], ex.at[gi, t], e_send.at[gi, t], e_recv.at[gi, t], at(chip - 1 if t == 0 else chip + 1, core))

    def send_terms(gi, j, t, total):
        low = total.astype(BF16)
        for k in range(2):
            ret_send[gi, j, t, k] = low[k * ROWS : (k + 1) * ROWS]
            ret_copy(gi, j, t, k).start()

    def own_swap(gi):
        return remote(own.at[gi, :, theirs], own_rx.at[gi], o_send.at[gi], o_recv.at[gi], sibling)

    def terms(gi, j):
        rows = slice(j * PAIR, (j + 1) * PAIR)
        dk = dv = None
        for e0 in range(0, GROUP, 2):
            low = []
            for e in range(e0, e0 + 2):
                p = w_s[gi, j, e] * l_s[gi, e, :1]
                ds_s[gi, rows, e * PAIR : (e + 1) * PAIR] = (p * (dp_s[gi, j, e] - d_s[gi, e, :1])).astype(BF16)
                low.append(p.astype(BF16))
            part = slice(e0 * PAIR, (e0 + 2) * PAIR)
            dv_part = dot(jnp.concatenate(low, axis=1), gh_s[gi, part], NN)
            dk_part = dot(ds_s[gi, rows, part], qh_s[gi, part], NN)
            dv = dv_part if dv is None else dv + dv_part
            dk = dk_part if dk is None else dk + dk_part
        return dk, dv

    def all_terms(gi, between=None):
        if gi in TERM_HOPS:
            for t, total in enumerate(terms(gi, 2)):
                ex_send[gi, t] = total.astype(BF16)
                ex_copy(gi, t).start()
            held[0], dv = terms(gi, 1)
            send_terms(gi, 1, 1, dv)
            if between is not None:
                between()
            dk, held[1] = terms(gi, 3)
            send_terms(gi, 3, 0, dk)
            for t in range(2):
                ex_copy(gi, t).wait_recv()
                send_terms(gi, (1, 3)[t], t, held[t] + ex[gi, t].astype(F32))
        else:
            for j in (1, 2, 3):
                for t, total in enumerate(terms(gi, j)):
                    send_terms(gi, j, t, total)
        own[gi, 0], own[gi, 1] = terms(gi, 0)
        own_swap(gi).start()

    def dq_local(gi):
        return pltpu.make_async_copy(dq_s.at[gi, mine], dq_hbm.at[:, query_cols(core, gi)], dq_sem.at[gi])

    def dq_swap(gi):
        return remote(dq_s.at[gi, theirs], dq_hbm.at[:, query_cols(core, gi)], dq_send.at[gi], dq_recv.at[gi], sibling)

    def query_grads(gi):
        def last(e, _):
            dqt = dot(kt_s[gi], ds_s[gi, :, pl.ds(pl.multiple_of(e * PAIR, PAIR), PAIR)], NN) * FACTOR
            dq_s[gi, :, head_cols(e)] = dqt.astype(BF16).T
            return 0

        lax.fori_loop(0, GROUP, last, 0, unroll=8)
        dq_local(gi).start()
        dq_swap(gi).start()

    weights(0, 0)
    forward_kv(0)
    weights(1, 0)
    hop_kv(0)
    forward_kv(1)
    weights(0, 1)
    weights(0, 3)
    weights(0, 2)
    stats(0)
    all_terms(0, lambda: hop_kv(1))
    for j in (1, 3, 2):
        weights(1, j)
    forward_ret(0)
    stats(1)
    all_terms(1)
    forward_ret(1)
    query_grads(0)
    query_grads(1)

    for gi in range(GROUPS):
        for h, mine_too in ((core, True), (other, False)):
            if mine_too:
                total = own[gi, :, mine]
            else:
                own_swap(gi).wait_recv()
                total = own_rx[gi]
            for j in (3, 1) if gi in TERM_HOPS else (2, 3, 1):
                for t in range(2):
                    ret_arrived(h, gi, j, t).wait_recv()
                total = total + ret[h, gi, j].astype(F32)
            out_s[0, :, group_cols(h, gi)] = (total[0] * FACTOR).astype(BF16)
            out_s[1, :, group_cols(h, gi)] = total[1].astype(BF16)
    outs = []
    for t, dst in enumerate((dk_hbm, dv_hbm)):
        cp = pltpu.make_async_copy(out_s.at[t], dst, out_sem.at[t])
        cp.start()
        outs.append(cp)
    for cp in outs:
        cp.wait()
    for gi in range(GROUPS):
        dq_local(gi).wait()
        dq_swap(gi).wait()
        own_swap(gi).wait_send()
        for t in range(2):
            q_swap(gi, t).wait_send()
            kv_swap(gi, t).wait_send()
            if gi in KV_HOPS:
                kv_hop(gi, t).wait_send()
            if gi in TERM_HOPS:
                ex_copy(gi, t).wait_send()
            for k in range(2):
                for j in (1, 3) if gi in KV_HOPS else (1, 2, 3):
                    kv_copy(gi, j, k, t).wait_send()
                for j in (1, 3) if gi in TERM_HOPS else (1, 2, 3):
                    ret_copy(gi, j, t, k).wait_send()

        @pl.when(py == 0)
        def _():
            for t in range(2):
                for k in range(2):
                    kv_forward(gi, t, k).wait_send()

        @pl.when(py == SIDE - 1)
        def _():
            for t in range(2):
                for h in range(2):
                    ret_forward(gi, t, h).wait_send()


def handed_on(dq, dk, dv, dq_out, dk_out, dv_out):
    dq_out[...] = dq[...]
    dk_out[...] = dk[...]
    dv_out[...] = dv[...]


def shards(queries, keys, values, grads, lengths):
    q, k, v, g = queries[0], keys[0], values[0], grads[0]
    vmem = pltpu.VMEM
    dma = pltpu.SemaphoreType.DMA
    hbm = pl.BlockSpec(memory_space=pl.ANY)
    dq, dk, dv = pl.pallas_call(
        kernel,
        out_shape=[jax.ShapeDtypeStruct(a.shape, BF16) for a in (q, k, v)],
        in_specs=[pl.BlockSpec(memory_space=pltpu.SMEM)] + [hbm] * 4,
        out_specs=[hbm] * 3,
        scratch_shapes=[
            vmem((GROUPS, PAIR, GROUP * HEAD), BF16),
            vmem((GROUPS, PAIR, GROUP * HEAD), BF16),
            vmem((GROUPS, GROUP, HEAD, PAIR), BF16),
            vmem((GROUPS, GROUP, HEAD, PAIR), BF16),
            vmem((GROUPS, GROUP * PAIR, HEAD), BF16),
            vmem((GROUPS, GROUP * PAIR, HEAD), BF16),
            vmem((2, GROUPS, 2, ROWS, HEAD), BF16),
            vmem((GROUPS, SLOTS + 1, 2, PAIR, HEAD), BF16),
            vmem((SLOTS, PAIR, PAIR), F32),
            vmem((GROUPS, SLOTS, GROUP, PAIR, PAIR), F32),
            vmem((GROUPS, SLOTS, GROUP, PAIR, PAIR), F32),
            vmem((GROUPS, GROUP, 8, PAIR), F32),
            vmem((GROUPS, GROUP, 8, PAIR), F32),
            vmem((GROUPS, SLOTS * PAIR, GROUP * PAIR), BF16),
            vmem((GROUPS, 2, PAIR, HEAD), BF16),
            vmem((GROUPS, 2, PAIR, HEAD), BF16),
            vmem((2, PAIR, HEAD), F32),
            vmem((GROUPS, SLOTS, 2, 2, ROWS, HEAD), BF16),
            vmem((2, GROUPS, SLOTS + 1, 2, ROWS, HEAD), BF16),
            vmem((GROUPS, 2, PAIR, HEAD), F32),
            vmem((GROUPS, 2, ROWS, HEAD), F32),
            vmem((2, ROWS, 2 * GROUPS * HEAD), BF16),
            vmem((GROUPS, PAIR, GROUP * HEAD), BF16),
            vmem((GROUPS, HEAD, SLOTS * PAIR), BF16),
            dma((GROUPS, 2)), dma((GROUPS, 2)), dma((GROUPS, 2)),
            dma((2, GROUPS, 2)), dma((GROUPS, 2)),
            dma((GROUPS, SLOTS, 2, 2)), dma((GROUPS, SLOTS + 1, 2, 2)), dma((GROUPS, 2, 2)), dma((GROUPS, 2)),
            dma((GROUPS, 2)), dma((GROUPS, 2)),
            dma((GROUPS, SLOTS, 2, 2)), dma((2, GROUPS, SLOTS + 1, 2)), dma((GROUPS, 2, 2)),
            dma((GROUPS,)), dma((GROUPS,)),
            dma((2,)), dma((GROUPS,)), dma((GROUPS,)), dma((GROUPS,)),
        ],
        compiler_params=pltpu.CompilerParams(
            collective_id=0, has_side_effects=True, vmem_limit_bytes=60 << 20
        ),
    )(lengths, q, k, v, g)
    steps = 2
    specs = [pl.BlockSpec((ROWS // steps, a.shape[1]), lambda i: (i, 0)) for a in (q, k, v)]
    dq, dk, dv = pl.pallas_call(
        handed_on, grid=(steps,), out_shape=[jax.ShapeDtypeStruct(a.shape, BF16) for a in (q, k, v)],
        in_specs=specs, out_specs=specs,
    )(dq, dk, dv)
    return dq[None], dk[None], dv[None]


def solution(mesh):
    spec = P("dp", "ctx", None)
    return jax.shard_map(
        shards,
        mesh=mesh,
        in_specs=(spec, spec, spec, spec, P()),
        out_specs=(spec, spec, spec),
        check_vma=False,
    )
```
